32 devices in a mesh: row: 4 (over z), col: 8 (over y, x, core).
Axes of the slice: x: 2, y: 2, z: 4, core: 2. Of those that a mesh axis runs over, the one named last changes fastest.
Arguments:
- values: bfloat16 [32, 8, 128, 128], P('row', 'col'), may hold values from -0.375 to 0.375
- column_slot_index: int32 [32, 8], P('row', 'col'), may hold values from 0 to 3
- branches: int32 [2], replicated, may hold values from 0 to 1, as said below
Outputs:
- purified: bfloat16 [32, 8, 128, 128], P('row', 'col')
The draws below stay inside these ranges and needn't reach their ends.
Inputs may be any that keep to these rules, and one draw needn't show every extreme that they name: column_slot_index[i, c] places block row i's single nonzero block among the 4 block columns of col index c. Branch 0 squares, branch 1 takes 2 X - X X; consecutive steps take different branches.
All inputs are finite; a program needn't handle non-finite values.
Results may differ from the reference program's by a relative error of at most 0.0051.
Values may be sent and summed in bfloat16 or wider, within the bound.
A program may use at most 64 MiB of HBM per device.

```python
import jax
import jax.numpy as jnp
from jax import lax

BS = 128
BPD = 4
STEPS = 2
NBR = 32
N_COL = 8


def draw_branches(key, part):
    key = jax.random.fold_in(key, 7)
    first = jax.random.randint(key, (1,), 0, 2, dtype=jnp.int32)
    return ((first + jnp.arange(STEPS, dtype=jnp.int32)) % 2).astype(jnp.int32)


def plant(drawn, key, low, top_value):
    longest = drawn.shape.index(max(drawn.shape))
    spots = []
    for shift in (0, 1):
        where = [jax.random.randint(jax.random.fold_in(key, axis), (), 0, length) for axis, length in enumerate(drawn.shape)]
        where[longest] = (where[longest] + shift) % drawn.shape[longest]
        spots.append(tuple(where))
    return drawn.at[spots[0]].set(low).at[spots[1]].set(top_value)


def block_scale(key, dims, cuts, smallest, high):
    level, own = 1.0, jax.random.fold_in(key, 6)
    for position, parts in cuts:
        draws = jnp.exp(jax.random.uniform(jax.random.fold_in(own, position), (parts,), jnp.float32, smallest / len(cuts), high / len(cuts)))
        level = level * jnp.repeat(draws, dims[position] // parts).reshape([-1 if axis == position else 1 for axis in range(len(dims))])
    return level


def normal_values(rng, extent, deviation, reach, cuts=(), kind=jnp.bfloat16):
    level = block_scale(rng, extent, cuts, -0.22, 0.18) if cuts else 1.0
    entries = jax.random.normal(rng, extent, jnp.float32) * deviation * level
    return jnp.minimum(jnp.maximum(entries, -reach), reach).astype(kind)


def setup_inputs(seed: int = 0) -> dict:
    key_of = jax.random.split(jax.random.key(seed), 4)
    values = normal_values(key_of[0], (NBR, N_COL, BS, BS), (BS * N_COL // BPD) ** -0.5, 0.375, ((0, 4), (1, 8)))
    column_slot_index = plant(jax.random.randint(key_of[1], (NBR, N_COL), 0, BPD), jax.random.fold_in(key_of[1], 1), 0, BPD - 1).astype(jnp.int32)
    branches = draw_branches(jax.random.fold_in(key_of[3], 71), 0)
    return {"values": values, "column_slot_index": column_slot_index, "branches": branches}


def reference(values, column_slot_index, branches):
    state = values
    for step in range(STEPS):
        def single_block_row(pair):
            row_vals, row_ids = pair
            desired_trace = jnp.arange(N_COL, dtype=jnp.int32) * BPD + row_ids.astype(jnp.int32)
            selected_blocks = state[desired_trace].astype(jnp.float32)
            match = column_slot_index[desired_trace] == row_ids[None, :]
            selected_blocks = jnp.where(match[:, :, None, None], selected_blocks, jnp.zeros_like(selected_blocks))
            return jnp.einsum('pab,pqbd->qad', row_vals.astype(jnp.float32), selected_blocks)
        matrix_square = lax.map(single_block_row, (state, column_slot_index))
        twice_density = 2.0 * state.astype(jnp.float32) - matrix_square
        newer = jnp.where(branches[step] == 1, twice_density, matrix_square)
        state = newer.astype(jnp.bfloat16)
    return state
```

```python
import functools

import jax
import jax.numpy as jnp
from jax import lax
from jax.experimental import pallas as pl
from jax.experimental.pallas import tpu as pltpu
from jax.sharding import PartitionSpec as P

BPD = 4
MESH = pl.DeviceIdType.MESH


def flip(index, bits):
    out, place = index, 1
    while place <= bits:
        if bits & place:
            out = out + place - 2 * place * lax.rem(lax.div(index, place), 2)
        place *= 2
    return out


def kernel(n, ncol, steps, branches, values, ids, out, *scratch):
    rows = values.shape[0]
    per = rows // BPD
    chips = ncol // 2
    bufs = [scratch[s * n:(s + 1) * n] for s in range(steps)]
    scratch = scratch[steps * n:]
    strips, scratch = scratch[:steps], scratch[steps:]
    (acc, own_ids, col_ids, strip_ids, col_s, strip_s,
     id_send, id_recv_z, id_recv_c, local_sem,
     z_send, z_recv, c_send, p_send, c_recv) = scratch

    z, c = lax.axis_index("row"), lax.axis_index("col")
    chip, core = lax.div(c, 2), lax.rem(c, 2)
    peer = c + 1 - 2 * core

    col_others = [lax.rem(c + j, ncol) for j in range(1, ncol)]
    row_others = [lax.rem(z + j, n) for j in range(1, n)]
    barrier = pltpu.get_barrier_semaphore()
    for other in col_others:
        pl.semaphore_signal(barrier, inc=1, device_id=(z, other), device_id_type=MESH)
    for other in row_others:
        pl.semaphore_signal(barrier, inc=1, device_id=(other, c), device_id_type=MESH)
    own_ids[...] = jnp.zeros_like(own_ids)
    own_ids[0:rows, :] = jnp.broadcast_to(ids[...], (rows, own_ids.shape[1]))
    pl.semaphore_wait(barrier, ncol + n - 2)

    def remote(src, dst, send, recv, device):
        return pltpu.make_async_remote_copy(
            src_ref=src, dst_ref=dst, send_sem=send, recv_sem=recv,
            device_id=device, device_id_type=MESH)

    def z_copy(step, d, down):
        src = values if step == 0 and d == 0 else bufs[step][d]
        at = d + 1 if down else (d - 1) % n
        return remote(
            src.at[0:rows], bufs[step][at % n].at[0:rows],
            z_send.at[step, 0 if down else 1, d], z_recv.at[step, at % n],
            (jnp.maximum(z - 1, 0) if down else jnp.minimum(z + 1, n - 1), c))

    def z_arrival(step, d):
        return remote(
            bufs[step][d].at[0:rows], bufs[step][d].at[0:rows],
            z_send.at[step, 0, d], z_recv.at[step, d], (z, peer))

    def c_copy(step, j):
        src = values.at[0:rows] if step == 0 else bufs[step][0].at[0:rows]
        return remote(src, strips[step].at[c], c_send.at[step, j], c_recv.at[step, c],
                      (z, flip(chip, j) * 2 + core if j else peer))

    def p_copy(step, j):
        origin = flip(chip, j) * 2 + core
        return remote(strips[step].at[origin], strips[step].at[origin],
                      p_send.at[step, j], c_recv.at[step, origin], (z, peer))

    def c_arrival(step, origin):
        return remote(strips[step].at[origin], strips[step].at[origin],
                      p_send.at[step, 0], c_recv.at[step, origin], (z, peer))

    def send_own(step):
        @pl.when(z > 0)
        def _():
            z_copy(step, 0, True).start()

        @pl.when(z < n - 1)
        def _():
            z_copy(step, 0, False).start()

        for j in list(range(1, chips)) + [0]:
            c_copy(step, j).start()

    def add(step, d, q):
        for i in range(rows):
            left, right = [], []
            for t in range(per):
                p = q * per + t
                slot = strip_s[p, i, 0]
                k = t * BPD + slot
                k = jnp.where(col_s[q, k, 0] == col_s[z, i, 0], k, rows)
                left.append(strips[step][p, i])
                right.append(bufs[step][d][k])
            term = jnp.dot(jnp.concatenate(left, 1), jnp.concatenate(right, 0),
                           preferred_element_type=jnp.float32)
            acc[i] = term if d == 0 else acc[i] + term

    sent_ids = []
    for t, other in enumerate(col_others):
        sent_ids.append(remote(own_ids, strip_ids.at[c], id_send.at[t], id_recv_c.at[c], (z, other)))
    for t, other in enumerate(row_others):
        sent_ids.append(remote(own_ids, col_ids.at[z], id_send.at[ncol - 1 + t], id_recv_z.at[z], (other, c)))
    send_own(0)
    for copy in sent_ids:
        copy.start()
    bufs[0][0][0:rows] = values[...]
    strips[0][c] = values[...]
    strip_ids[c] = own_ids[...]
    col_ids[z] = own_ids[...]
    for step in range(steps):
        for d in range(n):
            bufs[step][d][rows] = jnp.zeros(values.shape[1:], values.dtype)
    for other in col_others:
        remote(own_ids, strip_ids.at[other], id_send.at[0], id_recv_c.at[other], (z, other)).wait_recv()
    for other in row_others:
        remote(own_ids, col_ids.at[other], id_send.at[0], id_recv_z.at[other], (other, c)).wait_recv()
    to_strip = pltpu.make_async_copy(strip_ids, strip_s, local_sem.at[0])
    to_col = pltpu.make_async_copy(col_ids, col_s, local_sem.at[1])
    to_strip.start()
    to_col.start()
    to_strip.wait()
    to_col.wait()

    for step in range(steps):
        def take(m):
            @pl.when(z + m < n)
            def _():
                z_arrival(step, m).wait_recv()
                if m + 1 < n:
                    @pl.when(z > 0)
                    def _():
                        z_copy(step, m, True).start()

            @pl.when(z - m >= 0)
            def _():
                z_arrival(step, n - m).wait_recv()
                if m + 1 < n:
                    @pl.when(z < n - 1)
                    def _():
                        z_copy(step, n - m, False).start()

        def use(m):
            if m == 0:
                add(step, 0, z)
                return

            @pl.when(z + m < n)
            def _():
                add(step, m, z + m)

            @pl.when(z - m >= 0)
            def _():
                add(step, n - m, z - m)

        def take_col(js):
            for j in js:
                c_arrival(step, flip(chip, j) * 2 + core).wait_recv()
                p_copy(step, j).start()

        done = 0
        for m in range(1, n):
            take(m)
            if m == 1:
                take_col(range(1, min(3, chips)))
            if m == min(2, n - 1):
                take_col(range(3, chips))
                for j in range(chips):
                    c_arrival(step, flip(chip, j) * 2 + 1 - core).wait_recv()
                use(0)
                done = 1
            if done:
                while done < m:
                    use(done)
                    done += 1
        while done < n:
            use(done)
            done += 1

        branch = branches[step]
        for i in range(rows):
            old = bufs[step][0][i].astype(jnp.float32)
            total = acc[i]
            new = jnp.where(branch == 1, 2.0 * old - total, total).astype(values.dtype)
            if step == steps - 1:
                out[i] = new
            else:
                bufs[step + 1][0][i] = new
                strips[step + 1][c, i] = new
        if step < steps - 1:
            send_own(step + 1)

    for copy in sent_ids:
        copy.wait_send()
    for step in range(steps):
        for j in range(chips):
            c_copy(step, j).wait_send()
            if j:
                p_copy(step, j).wait_send()
        for d in range(n - 1):
            @pl.when((z > 0) & (z + d < n))
            def _():
                z_copy(step, d, True).wait_send()

            @pl.when((z < n - 1) & (z - d >= 0))
            def _():
                z_copy(step, (n - d) % n, False).wait_send()


def purify(n, ncol, values, column_slot_index, branches):
    rows, _, bs, _ = values.shape
    steps = branches.shape[0]
    block = (rows, bs, bs)
    id_rows = -(-rows // 8) * 8
    scratch = [pltpu.VMEM((rows + 1, bs, bs), values.dtype) for _ in range(steps * n)]
    scratch += [pltpu.VMEM((ncol,) + block, values.dtype) for _ in range(steps)]
    scratch += [
        pltpu.VMEM(block, jnp.float32),
        pltpu.VMEM((id_rows, 128), jnp.int32),
        pltpu.VMEM((n, id_rows, 128), jnp.int32),
        pltpu.VMEM((ncol, id_rows, 128), jnp.int32),
        pltpu.SMEM((n, id_rows, 128), jnp.int32),
        pltpu.SMEM((ncol, id_rows, 128), jnp.int32),
        pltpu.SemaphoreType.DMA((ncol + n - 2,)),
        pltpu.SemaphoreType.DMA((n,)),
        pltpu.SemaphoreType.DMA((ncol,)),
        pltpu.SemaphoreType.DMA((2,)),
        pltpu.SemaphoreType.DMA((steps, 2, n)),
        pltpu.SemaphoreType.DMA((steps, n)),
        pltpu.SemaphoreType.DMA((steps, ncol // 2)),
        pltpu.SemaphoreType.DMA((steps, ncol // 2)),
        pltpu.SemaphoreType.DMA((steps, ncol)),
    ]
    vmem = pl.BlockSpec(memory_space=pltpu.VMEM)
    new = pl.pallas_call(
        functools.partial(kernel, n, ncol, steps),
        out_shape=jax.ShapeDtypeStruct(block, values.dtype),
        in_specs=[pl.BlockSpec(memory_space=pltpu.SMEM), vmem, vmem],
        out_specs=vmem,
        scratch_shapes=scratch,
        compiler_params=pltpu.CompilerParams(
            collective_id=0, has_side_effects=True, vmem_limit_bytes=48 * 2**20),
    )(branches, values.reshape(block), column_slot_index)
    return new.reshape(values.shape)


def solution(mesh):
    in_specs = (P("row", "col", None, None), P("row", "col"), P())
    out_specs = P("row", "col", None, None)
    body = functools.partial(purify, mesh.shape["row"], mesh.shape["col"])
    return jax.shard_map(body, mesh=mesh, in_specs=in_specs, out_specs=out_specs, check_vma=False)
```

```python
import functools

import jax
import jax.numpy as jnp
from jax import lax
from jax.experimental import pallas as pl
from jax.experimental.pallas import tpu as pltpu
from jax.sharding import PartitionSpec as P

BPD = 4
PIECES = 4
MESH = pl.DeviceIdType.MESH


def flip(index, bits):
    out, place = index, 1
    while place <= bits:
        if bits & place:
            out = out + place - 2 * place * lax.rem(lax.div(index, place), 2)
        place *= 2
    return out


def kernel(n, ncol, steps, branches, values, ids, out, *scratch):
    rows = values.shape[0]
    per = rows // BPD
    part = rows // PIECES
    chips = ncol // 2
    bufs = [scratch[s * n:(s + 1) * n] for s in range(steps)]
    scratch = scratch[steps * n:]
    strips, scratch = scratch[:steps], scratch[steps:]
    (acc, ids_in, branch_s, own_ids, col_ids, strip_ids, col_s, strip_s,
     id_send, id_recv_z, id_recv_c, local_sem,
     z_send, z_recv, c_send, p_send, c_recv) = scratch

    z, c = lax.axis_index("row"), lax.axis_index("col")
    chip, core = lax.div(c, 2), lax.rem(c, 2)
    peer = c + 1 - 2 * core

    loads = [
        pltpu.make_async_copy(values, bufs[0][0].at[0:rows], local_sem.at[0]),
        pltpu.make_async_copy(values, strips[0].at[c], local_sem.at[1]),
        pltpu.make_async_copy(ids, ids_in, local_sem.at[2]),
        pltpu.make_async_copy(branches, branch_s, local_sem.at[3]),
    ]
    for load in loads:
        load.start()
    col_others = [lax.rem(c + j, ncol) for j in range(1, ncol)]
    row_others = [lax.rem(z + j, n) for j in range(1, n)]
    barrier = pltpu.get_barrier_semaphore()
    for other in col_others:
        pl.semaphore_signal(barrier, inc=1, device_id=(z, other), device_id_type=MESH)
    for other in row_others:
        pl.semaphore_signal(barrier, inc=1, device_id=(other, c), device_id_type=MESH)
    own_ids[...] = jnp.zeros_like(own_ids)
    for step in range(steps):
        for d in range(n):
            bufs[step][d][rows] = jnp.zeros(values.shape[1:], values.dtype)
    for load in loads:
        load.wait()
    own_ids[0:rows, :] = jnp.broadcast_to(ids_in[...], (rows, own_ids.shape[1]))
    strip_ids[c] = own_ids[...]
    col_ids[z] = own_ids[...]
    pl.semaphore_wait(barrier, ncol + n - 2)

    def remote(src, dst, send, recv, device):
        return pltpu.make_async_remote_copy(
            src_ref=src, dst_ref=dst, send_sem=send, recv_sem=recv,
            device_id=device, device_id_type=MESH)

    def z_copy(step, d, down, piece):
        at = d + 1 if down else (d - 1) % n
        span = pl.ds(piece * part, part)
        return remote(
            bufs[step][d].at[span], bufs[step][at].at[span],
            z_send.at[step, 0 if down else 1, d, piece], z_recv.at[step, at, piece],
            (jnp.maximum(z - 1, 0) if down else jnp.minimum(z + 1, n - 1), c))

    def z_arrival(step, d, piece):
        span = pl.ds(piece * part, part)
        return remote(
            bufs[step][d].at[span], bufs[step][d].at[span],
            z_send.at[step, 0, d, piece], z_recv.at[step, d, piece], (z, peer))

    def c_copy(step, j):
        src = bufs[step][0].at[0:rows]
        return remote(src, strips[step].at[c], c_send.at[step, j], c_recv.at[step, c],
                      (z, flip(chip, j) * 2 + core if j else peer))

    def p_copy(step, j):
        origin = flip(chip, j) * 2 + core
        return remote(strips[step].at[origin], strips[step].at[origin],
                      p_send.at[step, j], c_recv.at[step, origin], (z, peer))

    def c_arrival(step, origin):
        return remote(strips[step].at[origin], strips[step].at[origin],
                      p_send.at[step, 0], c_recv.at[step, origin], (z, peer))

    def send_own(step, piece):
        @pl.when(z > 0)
        def _():
            z_copy(step, 0, True, piece).start()

        @pl.when(z < n - 1)
        def _():
            z_copy(step, 0, False, piece).start()

    def send_col(step, js):
        for j in js:
            c_copy(step, j).start()

    near = list(range(1, min(3, chips))) + [0]
    far = list(range(3, chips))

    def add(step, d, q):
        for i in range(rows):
            left, right = [], []
            for t in range(per):
                p = q * per + t
                slot = strip_s[p, i, 0]
                k = t * BPD + slot
                k = jnp.where(col_s[q, k, 0] == col_s[z, i, 0], k, rows)
                left.append(strips[step][p, i])
                right.append(bufs[step][d][k])
            term = jnp.dot(jnp.concatenate(left, 1), jnp.concatenate(right, 0),
                           preferred_element_type=jnp.float32)
            acc[i] = term if d == 0 else acc[i] + term

    sent_ids = []
    for t, other in enumerate(col_others):
        sent_ids.append(remote(own_ids, strip_ids.at[c], id_send.at[t], id_recv_c.at[c], (z, other)))
    for t, other in enumerate(row_others):
        sent_ids.append(remote(own_ids, col_ids.at[z], id_send.at[ncol - 1 + t], id_recv_z.at[z], (other, c)))
    for copy in sent_ids:
        copy.start()
    for piece in range(PIECES):
        send_own(0, piece)
    send_col(0, near)

    def take_ids():
        for other in col_others:
            remote(own_ids, strip_ids.at[other], id_send.at[0], id_recv_c.at[other], (z, other)).wait_recv()
        for other in row_others:
            remote(own_ids, col_ids.at[other], id_send.at[0], id_recv_z.at[other], (other, c)).wait_recv()
        to_strip = pltpu.make_async_copy(strip_ids, strip_s, local_sem.at[0])
        to_col = pltpu.make_async_copy(col_ids, col_s, local_sem.at[1])
        to_strip.start()
        to_col.start()
        to_strip.wait()
        to_col.wait()

    for step in range(steps):
        def take(m, piece):
            @pl.when(z + m < n)
            def _():
                z_arrival(step, m, piece).wait_recv()
                if m + 1 < n:
                    @pl.when(z > 0)
                    def _():
                        z_copy(step, m, True, piece).start()

            @pl.when(z - m >= 0)
            def _():
                z_arrival(step, n - m, piece).wait_recv()
                if m + 1 < n:
                    @pl.when(z < n - 1)
                    def _():
                        z_copy(step, n - m, False, piece).start()

        def use(m):
            if m == 0:
                add(step, 0, z)
                return

            @pl.when(z + m < n)
            def _():
                add(step, m, z + m)

            @pl.when(z - m >= 0)
            def _():
                add(step, n - m, z - m)

        def take_col(js):
            for j in js:
                c_arrival(step, flip(chip, j) * 2 + core).wait_recv()
                p_copy(step, j).start()

        done = 0
        for m in range(1, n):
            for piece in range(PIECES):
                take(m, piece)
            if m == 1:
                send_col(step, far)
                take_col(near[:-1])
            if m == min(2, n - 1):
                take_col(far)
                if step == 0:
                    take_ids()
                for j in range(chips):
                    c_arrival(step, flip(chip, j) * 2 + 1 - core).wait_recv()
                use(0)
                done = 1
            if done:
                while done < m:
                    use(done)
                    done += 1
        while done < n:
            use(done)
            done += 1

        branch = branch_s[step]
        for i in range(rows):
            old = bufs[step][0][i].astype(jnp.float32)
            total = acc[i]
            new = jnp.where(branch == 1, 2.0 * old - total, total).astype(values.dtype)
            if step == steps - 1:
                out[i] = new
            else:
                bufs[step + 1][0][i] = new
                strips[step + 1][c, i] = new
                if (i + 1) % part == 0:
                    send_own(step + 1, i // part)
        if step < steps - 1:
            send_col(step + 1, near)

    for copy in sent_ids:
        copy.wait_send()
    for step in range(steps):
        for j in range(chips):
            c_copy(step, j).wait_send()
            if j:
                p_copy(step, j).wait_send()
        for d in range(n - 1):
            for piece in range(PIECES):
                @pl.when((z > 0) & (z + d < n))
                def _():
                    z_copy(step, d, True, piece).wait_send()

                @pl.when((z < n - 1) & (z - d >= 0))
                def _():
                    z_copy(step, (n - d) % n, False, piece).wait_send()


def purify(n, ncol, values, column_slot_index, branches):
    rows, _, bs, _ = values.shape
    steps = branches.shape[0]
    block = (rows, bs, bs)
    id_rows = -(-rows // 8) * 8
    scratch = [pltpu.VMEM((rows + 1, bs, bs), values.dtype) for _ in range(steps * n)]
    scratch += [pltpu.VMEM((ncol,) + block, values.dtype) for _ in range(steps)]
    scratch += [
        pltpu.VMEM(block, jnp.float32),
        pltpu.VMEM((rows, 1), jnp.int32),
        pltpu.SMEM((steps,), jnp.int32),
        pltpu.VMEM((id_rows, 128), jnp.int32),
        pltpu.VMEM((n, id_rows, 128), jnp.int32),
        pltpu.VMEM((ncol, id_rows, 128), jnp.int32),
        pltpu.SMEM((n, id_rows, 128), jnp.int32),
        pltpu.SMEM((ncol, id_rows, 128), jnp.int32),
        pltpu.SemaphoreType.DMA((ncol + n - 2,)),
        pltpu.SemaphoreType.DMA((n,)),
        pltpu.SemaphoreType.DMA((ncol,)),
        pltpu.SemaphoreType.DMA((4,)),
        pltpu.SemaphoreType.DMA((steps, 2, n, PIECES)),
        pltpu.SemaphoreType.DMA((steps, n, PIECES)),
        pltpu.SemaphoreType.DMA((steps, ncol // 2)),
        pltpu.SemaphoreType.DMA((steps, ncol // 2)),
        pltpu.SemaphoreType.DMA((steps, ncol)),
    ]
    vmem = pl.BlockSpec(memory_space=pltpu.VMEM)
    new = pl.pallas_call(
        functools.partial(kernel, n, ncol, steps),
        out_shape=jax.ShapeDtypeStruct(block, values.dtype),
        in_specs=[pl.BlockSpec(memory_space=pl.ANY)] * 3,
        out_specs=vmem,
        scratch_shapes=scratch,
        compiler_params=pltpu.CompilerParams(
            collective_id=0, has_side_effects=True, vmem_limit_bytes=48 * 2**20),
    )(branches, values.reshape(block), column_slot_index)
    return new.reshape(values.shape)


def solution(mesh):
    in_specs = (P("row", "col", None, None), P("row", "col"), P())
    out_specs = P("row", "col", None, None)
    body = functools.partial(purify, mesh.shape["row"], mesh.shape["col"])
    return jax.shard_map(body, mesh=mesh, in_specs=in_specs, out_specs=out_specs, check_vma=False)
```

```python
import functools

import jax
import jax.numpy as jnp
from jax import lax
from jax.experimental import pallas as pl
from jax.experimental.pallas import tpu as pltpu
from jax.sharding import PartitionSpec as P

BPD = 4
PIECES = 4
MESH = pl.DeviceIdType.MESH


def flip(index, bits):
    out, place = index, 1
    while place <= bits:
        if bits & place:
            out = out + place - 2 * place * lax.rem(lax.div(index, place), 2)
        place *= 2
    return out


def kernel(n, ncol, steps, branches, values, ids, out, *scratch):
    rows = values.shape[0]
    per = rows // BPD
    part = rows // PIECES
    chips = ncol // 2
    bufs = [scratch[s * n:(s + 1) * n] for s in range(steps)]
    scratch = scratch[steps * n:]
    strips, scratch = scratch[:steps], scratch[steps:]
    (acc, ids_in, branch_s, own_ids, col_ids, strip_ids, col_s, strip_s,
     id_send, id_recv_z, id_recv_c, local_sem,
     z_send, z_recv, c_send, p_send, d_send, c_recv) = scratch

    z, c = lax.axis_index("row"), lax.axis_index("col")
    chip, core = lax.div(c, 2), lax.rem(c, 2)
    peer = c + 1 - 2 * core

    loads = [
        pltpu.make_async_copy(values, bufs[0][0].at[0:rows], local_sem.at[0]),
        pltpu.make_async_copy(values, strips[0].at[c], local_sem.at[1]),
        pltpu.make_async_copy(ids, ids_in, local_sem.at[2]),
        pltpu.make_async_copy(branches, branch_s, local_sem.at[3]),
    ]
    for load in loads:
        load.start()
    col_others = [lax.rem(c + j, ncol) for j in range(1, ncol)]
    row_others = [lax.rem(z + j, n) for j in range(1, n)]
    barrier = pltpu.get_barrier_semaphore()
    for other in col_others:
        pl.semaphore_signal(barrier, inc=1, device_id=(z, other), device_id_type=MESH)
    for other in row_others:
        pl.semaphore_signal(barrier, inc=1, device_id=(other, c), device_id_type=MESH)
    own_ids[...] = jnp.zeros_like(own_ids)
    for step in range(steps):
        for d in range(n):
            bufs[step][d][rows] = jnp.zeros(values.shape[1:], values.dtype)
    for load in loads:
        load.wait()
    own_ids[0:rows, :] = jnp.broadcast_to(ids_in[...], (rows, own_ids.shape[1]))
    strip_ids[c] = own_ids[...]
    col_ids[z] = own_ids[...]
    pl.semaphore_wait(barrier, ncol + n - 2)

    def remote(src, dst, send, recv, device):
        return pltpu.make_async_remote_copy(
            src_ref=src, dst_ref=dst, send_sem=send, recv_sem=recv,
            device_id=device, device_id_type=MESH)

    def z_copy(step, d, down, piece):
        at = d + 1 if down else (d - 1) % n
        span = pl.ds(piece * part, part)
        return remote(
            bufs[step][d].at[span], bufs[step][at].at[span],
            z_send.at[step, 0 if down else 1, d, piece], z_recv.at[step, at, piece],
            (jnp.maximum(z - 1, 0) if down else jnp.minimum(z + 1, n - 1), c))

    def z_arrival(step, d, piece):
        span = pl.ds(piece * part, part)
        return remote(
            bufs[step][d].at[span], bufs[step][d].at[span],
            z_send.at[step, 0, d, piece], z_recv.at[step, d, piece], (z, peer))

    half = rows // 2

    def c_part(step, origin, h):
        return strips[step].at[origin, pl.ds(h * half, half)]

    def c_copy(step, j, h):
        src = bufs[step][0].at[pl.ds(h * half, half)]
        return remote(src, c_part(step, c, h), c_send.at[step, j, h], c_recv.at[step, c, h],
                      (z, flip(chip, j) * 2 + core if j else peer))

    def pass_on(step, j, h, to):
        origin = flip(chip, j) * 2 + core
        sem = p_send.at[step, j, h] if to == 0 else d_send.at[step, h]
        return remote(c_part(step, origin, h), c_part(step, origin, h), sem, c_recv.at[step, origin, h],
                      (z, flip(chip, to) * 2 + core if to else peer))

    def c_arrival(step, origin, h):
        return remote(c_part(step, origin, h), c_part(step, origin, h),
                      p_send.at[step, 0, h], c_recv.at[step, origin, h], (z, peer))

    def take_col(step, j, h):
        c_arrival(step, flip(chip, j) * 2 + core, h).wait_recv()
        if square and j == h + 1:
            pass_on(step, j, h, 2 - h).start()
        pass_on(step, j, h, 0).start()

    def send_own(step, piece):
        @pl.when(z > 0)
        def _():
            z_copy(step, 0, True, piece).start()

        @pl.when(z < n - 1)
        def _():
            z_copy(step, 0, False, piece).start()

    square = chips == 4
    near = list(range(1, min(3, chips)))
    far = list(range(3, chips))

    def send_col(step, h):
        for j in [0] + ([] if square else far):
            c_copy(step, j, h).start()
        for j in near:
            c_copy(step, j, h).start()

    def add(step, d, q):
        for i in range(rows):
            left, right = [], []
            for t in range(per):
                p = q * per + t
                slot = strip_s[p, i, 0]
                k = t * BPD + slot
                k = jnp.where(col_s[q, k, 0] == col_s[z, i, 0], k, rows)
                left.append(strips[step][p, i])
                right.append(bufs[step][d][k])
            term = jnp.dot(jnp.concatenate(left, 1), jnp.concatenate(right, 0),
                           preferred_element_type=jnp.float32)
            acc[i] = term if d == 0 else acc[i] + term

    sent_ids = []
    for t, other in enumerate(col_others):
        sent_ids.append(remote(own_ids, strip_ids.at[c], id_send.at[t], id_recv_c.at[c], (z, other)))
    for t, other in enumerate(row_others):
        sent_ids.append(remote(own_ids, col_ids.at[z], id_send.at[ncol - 1 + t], id_recv_z.at[z], (other, c)))
    for copy in sent_ids:
        copy.start()
    for piece in range(PIECES):
        send_own(0, piece)
    for h in range(2):
        send_col(0, h)

    def take_ids():
        for other in col_others:
            remote(own_ids, strip_ids.at[other], id_send.at[0], id_recv_c.at[other], (z, other)).wait_recv()
        for other in row_others:
            remote(own_ids, col_ids.at[other], id_send.at[0], id_recv_z.at[other], (other, c)).wait_recv()
        to_strip = pltpu.make_async_copy(strip_ids, strip_s, local_sem.at[0])
        to_col = pltpu.make_async_copy(col_ids, col_s, local_sem.at[1])
        to_strip.start()
        to_col.start()
        to_strip.wait()
        to_col.wait()

    for step in range(steps):
        def take(m, piece):
            @pl.when(z + m < n)
            def _():
                z_arrival(step, m, piece).wait_recv()
                if m + 1 < n:
                    @pl.when(z > 0)
                    def _():
                        z_copy(step, m, True, piece).start()

            @pl.when(z - m >= 0)
            def _():
                z_arrival(step, n - m, piece).wait_recv()
                if m + 1 < n:
                    @pl.when(z < n - 1)
                    def _():
                        z_copy(step, n - m, False, piece).start()

        def use(m):
            if m == 0:
                add(step, 0, z)
                return

            @pl.when(z + m < n)
            def _():
                add(step, m, z + m)

            @pl.when(z - m >= 0)
            def _():
                add(step, n - m, z - m)

        first, second = range(PIECES // 2), range(PIECES // 2, PIECES)
        for h, pieces in enumerate((first, second)):
            for piece in pieces:
                take(1, piece)
            for j in near:
                take_col(step, j, h)
        if n > 2:
            take(2, 0)
        for h in range(2):
            for j in far:
                take_col(step, j, h)
        if n > 2:
            take(2, 1)
        if step == 0:
            take_ids()
        for h in range(2):
            for j in range(chips):
                c_arrival(step, flip(chip, j) * 2 + 1 - core, h).wait_recv()
        use(0)
        if n > 2:
            take(2, 2)
        use(1)
        if n > 2:
            take(2, 3)
            use(2)
        for m in range(3, n):
            for piece in range(PIECES):
                take(m, piece)
            use(m)

        branch = branch_s[step]
        for i in range(rows):
            old = bufs[step][0][i].astype(jnp.float32)
            total = acc[i]
            new = jnp.where(branch == 1, 2.0 * old - total, total).astype(values.dtype)
            if step == steps - 1:
                out[i] = new
            else:
                bufs[step + 1][0][i] = new
                strips[step + 1][c, i] = new
                if (i + 1) % part == 0:
                    send_own(step + 1, i // part)
                if (i + 1) % half == 0:
                    send_col(step + 1, i // half)

    for copy in sent_ids:
        copy.wait_send()
    for step in range(steps):
        for h in range(2):
            for j in [0] + near + ([] if square else far):
                c_copy(step, j, h).wait_send()
            for j in range(1, chips):
                pass_on(step, j, h, 0).wait_send()
            if square:
                pass_on(step, h + 1, h, 2 - h).wait_send()
        for d in range(n - 1):
            for piece in range(PIECES):
                @pl.when((z > 0) & (z + d < n))
                def _():
                    z_copy(step, d, True, piece).wait_send()

                @pl.when((z < n - 1) & (z - d >= 0))
                def _():
                    z_copy(step, (n - d) % n, False, piece).wait_send()


def purify(n, ncol, values, column_slot_index, branches):
    rows, _, bs, _ = values.shape
    steps = branches.shape[0]
    block = (rows, bs, bs)
    id_rows = -(-rows // 8) * 8
    scratch = [pltpu.VMEM((rows + 1, bs, bs), values.dtype) for _ in range(steps * n)]
    scratch += [pltpu.VMEM((ncol,) + block, values.dtype) for _ in range(steps)]
    scratch += [
        pltpu.VMEM(block, jnp.float32),
        pltpu.VMEM((rows, 1), jnp.int32),
        pltpu.SMEM((steps,), jnp.int32),
        pltpu.VMEM((id_rows, 128), jnp.int32),
        pltpu.VMEM((n, id_rows, 128), jnp.int32),
        pltpu.VMEM((ncol, id_rows, 128), jnp.int32),
        pltpu.SMEM((n, id_rows, 128), jnp.int32),
        pltpu.SMEM((ncol, id_rows, 128), jnp.int32),
        pltpu.SemaphoreType.DMA((ncol + n - 2,)),
        pltpu.SemaphoreType.DMA((n,)),
        pltpu.SemaphoreType.DMA((ncol,)),
        pltpu.SemaphoreType.DMA((4,)),
        pltpu.SemaphoreType.DMA((steps, 2, n, PIECES)),
        pltpu.SemaphoreType.DMA((steps, n, PIECES)),
        pltpu.SemaphoreType.DMA((steps, ncol // 2, 2)),
        pltpu.SemaphoreType.DMA((steps, ncol // 2, 2)),
        pltpu.SemaphoreType.DMA((steps, 2)),
        pltpu.SemaphoreType.DMA((steps, ncol, 2)),
    ]
    vmem = pl.BlockSpec(memory_space=pltpu.VMEM)
    new = pl.pallas_call(
        functools.partial(kernel, n, ncol, steps),
        out_shape=jax.ShapeDtypeStruct(block, values.dtype),
        in_specs=[pl.BlockSpec(memory_space=pltpu.HBM)] * 3,
        out_specs=vmem,
        scratch_shapes=scratch,
        compiler_params=pltpu.CompilerParams(
            collective_id=0, has_side_effects=True, vmem_limit_bytes=48 * 2**20),
    )(branches, values.reshape(block), column_slot_index)
    return new.reshape(values.shape)


def solution(mesh):
    in_specs = (P("row", "col", None, None), P("row", "col"), P())
    out_specs = P("row", "col", None, None)
    body = functools.partial(purify, mesh.shape["row"], mesh.shape["col"])
    return jax.shard_map(body, mesh=mesh, in_specs=in_specs, out_specs=out_specs, check_vma=False)
```

```python
import functools

import jax
import jax.numpy as jnp
from jax import lax
from jax.experimental import pallas as pl
from jax.experimental.pallas import tpu as pltpu
from jax.sharding import PartitionSpec as P

BPD = 4
PIECES = 4
VMEM_LIMIT = 64 * 2**20 - 2**17
MESH = pl.DeviceIdType.MESH


def flip(index, bits):
    out, place = index, 1
    while place <= bits:
        if bits & place:
            out = out + place - 2 * place * lax.rem(lax.div(index, place), 2)
        place *= 2
    return out


def kernel(n, ncol, steps, branches, values, ids, out, *scratch):
    rows = values.shape[0]
    per = rows // BPD
    part = rows // PIECES
    chips = ncol // 2
    bufs = [scratch[s * n:(s + 1) * n] for s in range(steps)]
    scratch = scratch[steps * n:]
    strips, scratch = scratch[:steps], scratch[steps:]
    (acc, ids_in, branch_s, own_ids, col_ids, strip_ids, col_s, strip_s,
     id_send, id_recv_z, id_recv_c, local_sem,
     z_send, z_recv, c_send, p_send, d_send, c_recv) = scratch

    z, c = lax.axis_index("row"), lax.axis_index("col")
    chip, core = lax.div(c, 2), lax.rem(c, 2)
    peer = c + 1 - 2 * core

    loads = [
        pltpu.make_async_copy(values, bufs[0][0].at[0:rows], local_sem.at[0]),
        pltpu.make_async_copy(values, strips[0].at[c], local_sem.at[1]),
        pltpu.make_async_copy(ids, ids_in, local_sem.at[2]),
        pltpu.make_async_copy(branches, branch_s, local_sem.at[3]),
    ]
    for load in loads:
        load.start()
    col_others = [lax.rem(c + j, ncol) for j in range(1, ncol)]
    row_others = [lax.rem(z + j, n) for j in range(1, n)]
    barrier = pltpu.get_barrier_semaphore()
    for other in col_others:
        pl.semaphore_signal(barrier, inc=1, device_id=(z, other), device_id_type=MESH)
    for other in row_others:
        pl.semaphore_signal(barrier, inc=1, device_id=(other, c), device_id_type=MESH)
    own_ids[...] = jnp.zeros_like(own_ids)
    for step in range(steps):
        for d in range(n):
            bufs[step][d][rows] = jnp.zeros(values.shape[1:], values.dtype)
    for load in loads:
        load.wait()
    for i in range(rows):
        own_ids[i] = jnp.full(own_ids.shape[1:], ids_in[i], jnp.int32)
    strip_ids[c] = own_ids[...]
    col_ids[z] = own_ids[...]
    pl.semaphore_wait(barrier, ncol + n - 2)

    def remote(src, dst, send, recv, device):
        return pltpu.make_async_remote_copy(
            src_ref=src, dst_ref=dst, send_sem=send, recv_sem=recv,
            device_id=device, device_id_type=MESH)

    def z_copy(step, d, down, piece):
        at = d + 1 if down else (d - 1) % n
        span = pl.ds(piece * part, part)
        return remote(
            bufs[step][d].at[span], bufs[step][at].at[span],
            z_send.at[step, 0 if down else 1, d, piece], z_recv.at[step, at, piece],
            (jnp.maximum(z - 1, 0) if down else jnp.minimum(z + 1, n - 1), c))

    def z_arrival(step, d, piece):
        span = pl.ds(piece * part, part)
        return remote(
            bufs[step][d].at[span], bufs[step][d].at[span],
            z_send.at[step, 0, d, piece], z_recv.at[step, d, piece], (z, peer))

    half = rows // 2

    def c_part(step, origin, h):
        return strips[step].at[origin, pl.ds(h * half, half)]

    def c_copy(step, j, h):
        src = bufs[step][0].at[pl.ds(h * half, half)]
        return remote(src, c_part(step, c, h), c_send.at[step, j, h], c_recv.at[step, c, h],
                      (z, flip(chip, j) * 2 + core if j else peer))

    def pass_on(step, j, h, to):
        origin = flip(chip, j) * 2 + core
        sem = p_send.at[step, j, h] if to == 0 else d_send.at[step, h]
        return remote(c_part(step, origin, h), c_part(step, origin, h), sem, c_recv.at[step, origin, h],
                      (z, flip(chip, to) * 2 + core if to else peer))

    def c_arrival(step, origin, h):
        return remote(c_part(step, origin, h), c_part(step, origin, h),
                      p_send.at[step, 0, h], c_recv.at[step, origin, h], (z, peer))

    def take_col(step, j, h):
        c_arrival(step, flip(chip, j) * 2 + core, h).wait_recv()
        if square and j == h + 1:
            pass_on(step, j, h, 2 - h).start()
        pass_on(step, j, h, 0).start()

    def send_own(step, piece):
        @pl.when(z > 0)
        def _():
            z_copy(step, 0, True, piece).start()

        @pl.when(z < n - 1)
        def _():
            z_copy(step, 0, False, piece).start()

    square = chips == 4
    near = list(range(1, min(3, chips)))
    far = list(range(3, chips))

    def send_col(step, h):
        for j in [0] + ([] if square else far):
            c_copy(step, j, h).start()
        for j in near:
            c_copy(step, j, h).start()

    def add(step, d, q):
        for i in range(rows):
            left, right = [], []
            for t in range(per):
                p = q * per + t
                slot = strip_s[p, i, 0]
                k = t * BPD + slot
                k = jnp.where(col_s[q, k, 0] == col_s[z, i, 0], k, rows)
                left.append(strips[step][p, i])
                right.append(bufs[step][d][k])
            term = jnp.dot(jnp.concatenate(left, 1), jnp.concatenate(right, 0),
                           preferred_element_type=jnp.float32)
            acc[i] = term if d == 0 else acc[i] + term

    sent_ids = []
    for t, other in enumerate(col_others):
        sent_ids.append(remote(own_ids, strip_ids.at[c], id_send.at[t], id_recv_c.at[c], (z, other)))
    for t, other in enumerate(row_others):
        sent_ids.append(remote(own_ids, col_ids.at[z], id_send.at[ncol - 1 + t], id_recv_z.at[z], (other, c)))
    for copy in sent_ids:
        copy.start()
    for piece in range(PIECES):
        send_own(0, piece)
    for h in range(2):
        send_col(0, h)

    def take_ids():
        for other in col_others:
            remote(own_ids, strip_ids.at[other], id_send.at[0], id_recv_c.at[other], (z, other)).wait_recv()
        for other in row_others:
            remote(own_ids, col_ids.at[other], id_send.at[0], id_recv_z.at[other], (other, c)).wait_recv()
        to_strip = pltpu.make_async_copy(strip_ids, strip_s, local_sem.at[0])
        to_col = pltpu.make_async_copy(col_ids, col_s, local_sem.at[1])
        to_strip.start()
        to_col.start()
        to_strip.wait()
        to_col.wait()

    for step in range(steps):
        def take(m, piece):
            @pl.when(z + m < n)
            def _():
                z_arrival(step, m, piece).wait_recv()
                if m + 1 < n:
                    @pl.when(z > 0)
                    def _():
                        z_copy(step, m, True, piece).start()

            @pl.when(z - m >= 0)
            def _():
                z_arrival(step, n - m, piece).wait_recv()
                if m + 1 < n:
                    @pl.when(z < n - 1)
                    def _():
                        z_copy(step, n - m, False, piece).start()

        def use(m):
            if m == 0:
                add(step, 0, z)
                return

            @pl.when(z + m < n)
            def _():
                add(step, m, z + m)

            @pl.when(z - m >= 0)
            def _():
                add(step, n - m, z - m)

        first, second = range(PIECES // 2), range(PIECES // 2, PIECES)
        for h, pieces in enumerate((first, second)):
            for piece in pieces:
                take(1, piece)
            for j in near:
                take_col(step, j, h)
        if n > 2:
            take(2, 0)
        for h in range(2):
            for j in far:
                take_col(step, j, h)
        if n > 2:
            take(2, 1)
        if step == 0:
            take_ids()
        for h in range(2):
            for j in range(chips):
                c_arrival(step, flip(chip, j) * 2 + 1 - core, h).wait_recv()
        use(0)
        if n > 2:
            take(2, 2)
        use(1)
        if n > 2:
            take(2, 3)
            use(2)
        for m in range(3, n):
            for piece in range(PIECES):
                take(m, piece)
            use(m)

        branch = branch_s[step]
        for i in range(rows):
            old = bufs[step][0][i].astype(jnp.float32)
            total = acc[i]
            new = jnp.where(branch == 1, 2.0 * old - total, total).astype(values.dtype)
            if step == steps - 1:
                out[i] = new
            else:
                bufs[step + 1][0][i] = new
                strips[step + 1][c, i] = new
                if (i + 1) % part == 0:
                    send_own(step + 1, i // part)
                if (i + 1) % half == 0:
                    send_col(step + 1, i // half)

    for copy in sent_ids:
        copy.wait_send()
    for step in range(steps):
        for h in range(2):
            for j in [0] + near + ([] if square else far):
                c_copy(step, j, h).wait_send()
            for j in range(1, chips):
                pass_on(step, j, h, 0).wait_send()
            if square:
                pass_on(step, h + 1, h, 2 - h).wait_send()
        for d in range(n - 1):
            for piece in range(PIECES):
                @pl.when((z > 0) & (z + d < n))
                def _():
                    z_copy(step, d, True, piece).wait_send()

                @pl.when((z < n - 1) & (z - d >= 0))
                def _():
                    z_copy(step, (n - d) % n, False, piece).wait_send()


def purify(n, ncol, values, column_slot_index, branches):
    rows, _, bs, _ = values.shape
    steps = branches.shape[0]
    block = (rows, bs, bs)
    id_rows = -(-rows // 8) * 8
    scratch = [pltpu.VMEM((rows + 1, bs, bs), values.dtype) for _ in range(steps * n)]
    scratch += [pltpu.VMEM((ncol,) + block, values.dtype) for _ in range(steps)]
    scratch += [
        pltpu.VMEM(block, jnp.float32),
        pltpu.SMEM((rows,), jnp.int32),
        pltpu.SMEM((steps,), jnp.int32),
        pltpu.VMEM((id_rows, 128), jnp.int32),
        pltpu.VMEM((n, id_rows, 128), jnp.int32),
        pltpu.VMEM((ncol, id_rows, 128), jnp.int32),
        pltpu.SMEM((n, id_rows, 128), jnp.int32),
        pltpu.SMEM((ncol, id_rows, 128), jnp.int32),
        pltpu.SemaphoreType.DMA((ncol + n - 2,)),
        pltpu.SemaphoreType.DMA((n,)),
        pltpu.SemaphoreType.DMA((ncol,)),
        pltpu.SemaphoreType.DMA((4,)),
        pltpu.SemaphoreType.DMA((steps, 2, n, PIECES)),
        pltpu.SemaphoreType.DMA((steps, n, PIECES)),
        pltpu.SemaphoreType.DMA((steps, ncol // 2, 2)),
        pltpu.SemaphoreType.DMA((steps, ncol // 2, 2)),
        pltpu.SemaphoreType.DMA((steps, 2)),
        pltpu.SemaphoreType.DMA((steps, ncol, 2)),
    ]
    vmem = pl.BlockSpec(memory_space=pltpu.VMEM)
    new = pl.pallas_call(
        functools.partial(kernel, n, ncol, steps),
        out_shape=jax.ShapeDtypeStruct(block, values.dtype),
        in_specs=[pl.BlockSpec(memory_space=pltpu.HBM)] * 3,
        out_specs=vmem,
        scratch_shapes=scratch,
        compiler_params=pltpu.CompilerParams(
            collective_id=0, has_side_effects=True, vmem_limit_bytes=VMEM_LIMIT),
    )(branches, values.reshape(block), column_slot_index.reshape(rows))
    return new.reshape(values.shape)


def solution(mesh):
    in_specs = (P("row", "col", None, None), P("row", "col"), P())
    out_specs = P("row", "col", None, None)
    body = functools.partial(purify, mesh.shape["row"], mesh.shape["col"])
    return jax.shard_map(body, mesh=mesh, in_specs=in_specs, out_specs=out_specs, check_vma=False)
```

```python
import functools

import jax
import jax.numpy as jnp
from jax import lax
from jax.experimental import pallas as pl
from jax.experimental.pallas import tpu as pltpu
from jax.sharding import PartitionSpec as P

BPD = 4
PIECES = 4
VMEM_LIMIT = 64 * 2**20 - 2**17 - 2**18
MESH = pl.DeviceIdType.MESH


def flip(index, bits):
    out, place = index, 1
    while place <= bits:
        if bits & place:
            out = out + place - 2 * place * lax.rem(lax.div(index, place), 2)
        place *= 2
    return out


def kernel(n, ncol, steps, branches, values, ids, out, *scratch):
    rows = values.shape[0]
    per = rows // BPD
    part = rows // PIECES
    chips = ncol // 2
    bufs = [[scratch[(s * n + d) * per:(s * n + d + 1) * per] for d in range(n)] for s in range(steps)]
    scratch = scratch[steps * n * per:]
    strips, scratch = scratch[:steps], scratch[steps:]
    (acc, ids_in, branch_s, own_ids, col_ids, strip_ids, col_s, strip_s,
     id_send, id_recv_z, id_recv_c, local_sem,
     z_send, z_recv, c_send, p_send, d_send, c_recv) = scratch

    z, c = lax.axis_index("row"), lax.axis_index("col")
    chip, core = lax.div(c, 2), lax.rem(c, 2)
    peer = c + 1 - 2 * core

    def blocks(step, d, start, size):
        return bufs[step][d][start // BPD].at[pl.ds(start % BPD, size)]

    loads = [
        pltpu.make_async_copy(values.at[pl.ds(t * BPD, BPD)], bufs[0][0][t].at[0:BPD], local_sem.at[4 + t])
        for t in range(per)
    ] + [
        pltpu.make_async_copy(values, strips[0].at[c], local_sem.at[1]),
        pltpu.make_async_copy(ids, ids_in, local_sem.at[2]),
        pltpu.make_async_copy(branches, branch_s, local_sem.at[3]),
    ]
    for load in loads:
        load.start()
    col_others = [lax.rem(c + j, ncol) for j in range(1, ncol)]
    row_others = [lax.rem(z + j, n) for j in range(1, n)]
    barrier = pltpu.get_barrier_semaphore()
    for other in col_others:
        pl.semaphore_signal(barrier, inc=1, device_id=(z, other), device_id_type=MESH)
    for other in row_others:
        pl.semaphore_signal(barrier, inc=1, device_id=(other, c), device_id_type=MESH)
    own_ids[...] = jnp.zeros_like(own_ids)
    for step in range(steps):
        for d in range(n):
            for t in range(per):
                bufs[step][d][t][BPD] = jnp.zeros(values.shape[1:], values.dtype)
    for load in loads:
        load.wait()
    for i in range(rows):
        own_ids[i] = jnp.full(own_ids.shape[1:], ids_in[i], jnp.int32)
    strip_ids[c] = own_ids[...]
    col_ids[z] = own_ids[...]
    pl.semaphore_wait(barrier, ncol + n - 2)

    def remote(src, dst, send, recv, device):
        return pltpu.make_async_remote_copy(
            src_ref=src, dst_ref=dst, send_sem=send, recv_sem=recv,
            device_id=device, device_id_type=MESH)

    def z_copy(step, d, down, piece):
        at = d + 1 if down else (d - 1) % n
        return remote(
            blocks(step, d, piece * part, part), blocks(step, at, piece * part, part),
            z_send.at[step, 0 if down else 1, d, piece], z_recv.at[step, at, piece],
            (jnp.maximum(z - 1, 0) if down else jnp.minimum(z + 1, n - 1), c))

    def z_arrival(step, d, piece):
        span = blocks(step, d, piece * part, part)
        return remote(
            span, span,
            z_send.at[step, 0, d, piece], z_recv.at[step, d, piece], (z, peer))

    half = rows // 2

    def c_part(step, origin, h):
        return strips[step].at[origin, pl.ds(h * half, half)]

    def c_copy(step, j, h):
        src = blocks(step, 0, h * half, half)
        return remote(src, c_part(step, c, h), c_send.at[step, j, h], c_recv.at[step, c, h],
                      (z, flip(chip, j) * 2 + core if j else peer))

    def pass_on(step, j, h, to):
        origin = flip(chip, j) * 2 + core
        sem = p_send.at[step, j, h] if to == 0 else d_send.at[step, h]
        return remote(c_part(step, origin, h), c_part(step, origin, h), sem, c_recv.at[step, origin, h],
                      (z, flip(chip, to) * 2 + core if to else peer))

    def c_arrival(step, origin, h):
        return remote(c_part(step, origin, h), c_part(step, origin, h),
                      p_send.at[step, 0, h], c_recv.at[step, origin, h], (z, peer))

    def take_col(step, j, h):
        c_arrival(step, flip(chip, j) * 2 + core, h).wait_recv()
        if square and j == h + 1:
            pass_on(step, j, h, 2 - h).start()
        pass_on(step, j, h, 0).start()

    def send_own(step, piece):
        @pl.when(z > 0)
        def _():
            z_copy(step, 0, True, piece).start()

        @pl.when(z < n - 1)
        def _():
            z_copy(step, 0, False, piece).start()

    square = chips == 4
    near = list(range(1, min(3, chips)))
    far = list(range(3, chips))

    def send_col(step, h):
        for j in [0] + ([] if square else far):
            c_copy(step, j, h).start()
        for j in near:
            c_copy(step, j, h).start()

    def add(step, d, q, ts):
        for i in range(rows):
            left, right = [], []
            for t in ts:
                p = q * per + t
                k = strip_s[p, i, 0]
                k = jnp.where(col_s[q, t * BPD + k, 0] == col_s[z, i, 0], k, BPD)
                left.append(strips[step][p, i])
                right.append(bufs[step][d][t][k])
            term = jnp.dot(jnp.concatenate(left, 1), jnp.concatenate(right, 0),
                           preferred_element_type=jnp.float32)
            acc[i] = term if d == 0 else acc[i] + term

    sent_ids = []
    for t, other in enumerate(col_others):
        sent_ids.append(remote(own_ids, strip_ids.at[c], id_send.at[t], id_recv_c.at[c], (z, other)))
    for t, other in enumerate(row_others):
        sent_ids.append(remote(own_ids, col_ids.at[z], id_send.at[ncol - 1 + t], id_recv_z.at[z], (other, c)))
    for copy in sent_ids:
        copy.start()
    for piece in range(PIECES):
        send_own(0, piece)
    for h in range(2):
        send_col(0, h)

    def take_ids():
        for other in col_others:
            remote(own_ids, strip_ids.at[other], id_send.at[0], id_recv_c.at[other], (z, other)).wait_recv()
        for other in row_others:
            remote(own_ids, col_ids.at[other], id_send.at[0], id_recv_z.at[other], (other, c)).wait_recv()
        to_strip = pltpu.make_async_copy(strip_ids, strip_s, local_sem.at[0])
        to_col = pltpu.make_async_copy(col_ids, col_s, local_sem.at[1])
        to_strip.start()
        to_col.start()
        to_strip.wait()
        to_col.wait()

    for step in range(steps):
        def take(m, piece):
            @pl.when(z + m < n)
            def _():
                z_arrival(step, m, piece).wait_recv()
                if m + 1 < n:
                    @pl.when(z > 0)
                    def _():
                        z_copy(step, m, True, piece).start()

            @pl.when(z - m >= 0)
            def _():
                z_arrival(step, n - m, piece).wait_recv()
                if m + 1 < n:
                    @pl.when(z < n - 1)
                    def _():
                        z_copy(step, n - m, False, piece).start()

        def use(m, ts=range(per)):
            if m == 0:
                add(step, 0, z, ts)
                return

            @pl.when(z + m < n)
            def _():
                add(step, m, z + m, ts)

            @pl.when(z - m >= 0)
            def _():
                add(step, n - m, z - m, ts)

        first, second = range(PIECES // 2), range(PIECES // 2, PIECES)
        for h, pieces in enumerate((first, second)):
            for piece in pieces:
                take(1, piece)
            for j in near:
                take_col(step, j, h)
        if n > 2:
            take(2, 0)
        for h in range(2):
            for j in far:
                take_col(step, j, h)
        if n > 2:
            take(2, 1)
        if step == 0:
            take_ids()
        for h in range(2):
            for j in range(chips):
                c_arrival(step, flip(chip, j) * 2 + 1 - core, h).wait_recv()
        use(0)
        if n > 2:
            take(2, 2)
        use(1)
        if n > 2:
            take(2, 3)
            use(2)
        for m in range(3, n):
            for t in range(per):
                for piece in range(t * PIECES // per, (t + 1) * PIECES // per):
                    take(m, piece)
                if m == n - 1:
                    use(m, [t])
            if m < n - 1:
                use(m)

        branch = branch_s[step]
        for i in range(rows):
            old = bufs[step][0][i // BPD][i % BPD].astype(jnp.float32)
            total = acc[i]
            new = jnp.where(branch == 1, 2.0 * old - total, total).astype(values.dtype)
            if step == steps - 1:
                out[i] = new
            else:
                bufs[step + 1][0][i // BPD][i % BPD] = new
                strips[step + 1][c, i] = new
                if (i + 1) % part == 0:
                    send_own(step + 1, i // part)
                if (i + 1) % half == 0:
                    send_col(step + 1, i // half)

    for copy in sent_ids:
        copy.wait_send()
    for step in range(steps):
        for h in range(2):
            for j in [0] + near + ([] if square else far):
                c_copy(step, j, h).wait_send()
            for j in range(1, chips):
                pass_on(step, j, h, 0).wait_send()
            if square:
                pass_on(step, h + 1, h, 2 - h).wait_send()
        for d in range(n - 1):
            for piece in range(PIECES):
                @pl.when((z > 0) & (z + d < n))
                def _():
                    z_copy(step, d, True, piece).wait_send()

                @pl.when((z < n - 1) & (z - d >= 0))
                def _():
                    z_copy(step, (n - d) % n, False, piece).wait_send()


def purify(n, ncol, values, column_slot_index, branches):
    rows, _, bs, _ = values.shape
    steps = branches.shape[0]
    block = (rows, bs, bs)
    id_rows = -(-rows // 8) * 8
    scratch = [pltpu.VMEM((BPD + 1, bs, bs), values.dtype) for _ in range(steps * n * (rows // BPD))]
    scratch += [pltpu.VMEM((ncol,) + block, values.dtype) for _ in range(steps)]
    scratch += [
        pltpu.VMEM(block, jnp.float32),
        pltpu.SMEM((rows,), jnp.int32),
        pltpu.SMEM((steps,), jnp.int32),
        pltpu.VMEM((id_rows, 128), jnp.int32),
        pltpu.VMEM((n, id_rows, 128), jnp.int32),
        pltpu.VMEM((ncol, id_rows, 128), jnp.int32),
        pltpu.SMEM((n, id_rows, 128), jnp.int32),
        pltpu.SMEM((ncol, id_rows, 128), jnp.int32),
        pltpu.SemaphoreType.DMA((ncol + n - 2,)),
        pltpu.SemaphoreType.DMA((n,)),
        pltpu.SemaphoreType.DMA((ncol,)),
        pltpu.SemaphoreType.DMA((4 + rows // BPD,)),
        pltpu.SemaphoreType.DMA((steps, 2, n, PIECES)),
        pltpu.SemaphoreType.DMA((steps, n, PIECES)),
        pltpu.SemaphoreType.DMA((steps, ncol // 2, 2)),
        pltpu.SemaphoreType.DMA((steps, ncol // 2, 2)),
        pltpu.SemaphoreType.DMA((steps, 2)),
        pltpu.SemaphoreType.DMA((steps, ncol, 2)),
    ]
    vmem = pl.BlockSpec(memory_space=pltpu.VMEM)
    new = pl.pallas_call(
        functools.partial(kernel, n, ncol, steps),
        out_shape=pltpu.VMEM(block, values.dtype),
        in_specs=[pl.BlockSpec(memory_space=pltpu.HBM)] * 3,
        out_specs=vmem,
        scratch_shapes=scratch,
        compiler_params=pltpu.CompilerParams(
            collective_id=0, has_side_effects=True, vmem_limit_bytes=VMEM_LIMIT),
    )(branches, values.reshape(block), column_slot_index.reshape(rows))
    return new.reshape(values.shape)


def solution(mesh):
    in_specs = (P("row", "col", None, None), P("row", "col"), P())
    out_specs = P("row", "col", None, None)
    body = functools.partial(purify, mesh.shape["row"], mesh.shape["col"])
    return jax.shard_map(body, mesh=mesh, in_specs=in_specs, out_specs=out_specs, check_vma=False)
```
